128 devices in a mesh: dp: 8 (over y, core), expert: 16 (over x, z).
Axes of the slice: x: 4, y: 4, z: 4, core: 2. Of those that a mesh axis runs over, the one named last changes fastest.
Arguments:
- grad_parts: bfloat16 [8, 64, 768, 2048], P('dp', None, 'expert'), may hold values from -80 to 80, as said below
- momentum: float32 [128, 768, 1024], P(('dp', 'expert')), may hold values from -6 to 6
Outputs:
- update: bfloat16 [64, 768, 2048], P(None, 'expert', 'dp')
- new_momentum: float32 [128, 768, 1024], P(('dp', 'expert'))
The draws below stay inside these ranges and needn't reach their ends.
Inputs may be any that keep to these rules, and one draw needn't show every extreme that they name: `grad_parts`: real-valued gradient partials.
All inputs are finite; a program needn't handle non-finite values.
Results may differ from the reference program's by a relative error of at most 0.00105.
Values may be sent and summed in bfloat16 or wider, within the bound.
No kernel may reach another device: no remote copies, remote signals or barrier semaphores. Data moves between devices by JAX's collectives and lax.ppermute only.
A program may use at most 128 MiB of HBM per device.

```python
import math
import jax
import jax.numpy as jnp
from jax import lax

D = 2048
HID = 768
ITERS = 3
MATS = 64
N_DP = 8


def draw_grad_parts(key, part):
    key = jax.random.fold_in(key, 11)
    keys = jax.random.split(key, 4)
    col_scale = jnp.exp(jax.random.uniform(keys[0], (MATS, 1, D), jnp.float32, math.log(0.3), math.log(3.0)))
    row_scale = jnp.exp(jax.random.uniform(keys[1], (MATS, HID, 1), jnp.float32, math.log(0.5), math.log(2.0)))
    half_scale = jnp.exp(jax.random.uniform(keys[2], (MATS, 1, 2, 1), jnp.float32, math.log(0.35), math.log(2.8)))
    half_scale = jnp.broadcast_to(half_scale, (MATS, 1, 2, D // 2)).reshape(MATS, 1, D)
    noise = jnp.clip(jax.random.normal(keys[3], (N_DP, MATS, HID, D), jnp.float32), -4.0, 4.0)
    values = noise * col_scale[None] * row_scale[None] * half_scale[None]
    return values.astype(jnp.bfloat16)


def block_levels(key, shape, cuts, least, top_value):
    factor_of = 1.0
    for axis_at, parts in cuts:
        steps = jax.random.uniform(jax.random.fold_in(jax.random.fold_in(key, 6), axis_at), (parts,), jnp.float32, least / len(cuts), top_value / len(cuts))
        factor_of = factor_of * jnp.repeat(jnp.exp(steps), shape[axis_at] // parts).reshape((-1,) + (1,) * (len(shape) - 1 - axis_at))
    return factor_of


def bell_draw(own_key, shape, deviation, bound, shards=(), held_as=jnp.bfloat16):
    array = jax.random.normal(own_key, shape, jnp.float32) * deviation
    if len(shards) > 0:
        array = block_levels(own_key, shape, shards, -0.22, 0.18) * array
    return jnp.clip(array, min=-bound, max=bound).astype(held_as)


def setup_inputs(seed: int = 0) -> dict:
    key_list = jax.random.split(jax.random.key(seed), 3)
    grad_parts = draw_grad_parts(jax.random.fold_in(key_list[2], 71), 0)
    momentum = bell_draw(key_list[1], (2 * MATS, HID, D // 2), 1.0, 6.0, ((0, 128),), jnp.float32)
    return {"grad_parts": grad_parts, "momentum": momentum}


decay_rate = 0.95
norm_epsilon = 1e-07
rms_match = 0.2
lin_term = 3.4445
sq_term = -4.775
cube_term = 2.0315

def product(left, right):
    return jnp.dot(left, right, precision=lax.Precision.HIGHEST, preferred_element_type=jnp.float32)

def newton_schulz(matrix):
    total = jnp.sqrt(jnp.sum(matrix * matrix))
    current = matrix / (total + norm_epsilon)
    for sweep_index in range(ITERS):
        gram_block = product(current, current.T)
        poly = sq_term * gram_block + cube_term * product(gram_block, gram_block)
        current = lin_term * current + product(poly, current)
    scaled = rms_match * math.sqrt(max(HID, D)) * current
    return scaled.astype(jnp.bfloat16)

def reference(grad_parts, momentum):
    summed = jnp.zeros((MATS, HID, D), jnp.float32)
    for part_index in range(N_DP):
        summed = summed + grad_parts[part_index].astype(jnp.float32)
    previous = momentum.reshape(MATS, 2, HID, D // 2).transpose(0, 2, 1, 3).reshape(MATS, HID, D)
    renewed = decay_rate * previous + summed
    nesterov = summed + decay_rate * renewed
    update = lax.map(newton_schulz, nesterov)
    new_momentum = renewed.reshape(MATS, HID, 2, D // 2).transpose(0, 2, 1, 3).reshape(2 * MATS, HID, D // 2)
    return (update, new_momentum)
```

```python
import functools
import math

import jax
import jax.numpy as jnp
from jax import lax
from jax.experimental import pallas as pl
from jax.experimental.pallas import tpu as pltpu
from jax.sharding import PartitionSpec as P

D = 2048
HID = 768
HALF = D // 2
ROWS = 48
LANES = 128

decay_rate = 0.95
norm_epsilon = 1e-07
rms_match = 0.2
lin_term = 3.4445
sq_term = -4.775
cube_term = 2.0315

WIDTHS = (256, 256, 256, 256)
OFFSETS = tuple(sum(WIDTHS[:c]) for c in range(len(WIDTHS)))

F32 = jnp.float32
BF16 = jnp.bfloat16
MIB = 1 << 20


def call(kernel, inputs, in_specs, out_specs, out_shape, name,
         after=(), grid=(), where=None, aliases=None, scratch=(), micros=2.0):
    n, extra, outs = len(inputs), len(after), len(out_shape)
    lead = 0 if where is None else 1

    def run(*refs):
        first = lead + n + extra
        refs[first + outs][...] = jnp.zeros((8, LANES), F32)
        kernel(*refs[: lead + n], *refs[first : first + outs], *refs[first + outs + 1 :])

    spec = pltpu.PrefetchScalarGridSpec(
        num_scalar_prefetch=lead,
        grid=grid,
        in_specs=list(in_specs) + [pl.BlockSpec(memory_space=pl.ANY)] * extra,
        out_specs=list(out_specs) + [pl.BlockSpec((8, LANES), lambda *_: (0, 0))],
        scratch_shapes=scratch,
    )
    return pl.pallas_call(
        run,
        grid_spec=spec,
        out_shape=list(out_shape) + [jax.ShapeDtypeStruct((8, LANES), F32)],
        input_output_aliases={lead + k: v for k, v in (aliases or {}).items()},
        compiler_params=pltpu.CompilerParams(vmem_limit_bytes=50 * MIB),
        cost_estimate=pl.CostEstimate(
            flops=0, bytes_accessed=int(micros * 10), transcendentals=0
        ),
        name=name,
    )(*(() if where is None else (where,)), *inputs, *after)


def split(x):
    high = x.astype(BF16)
    return high, (x - high.astype(F32)).astype(BF16)


NN = (((1,), (0,)), ((), ()))
NT = (((1,), (1,)), ((), ()))


def dot3(ah, al, bh, bl, dims):
    dot = functools.partial(lax.dot_general, dimension_numbers=dims, preferred_element_type=F32)
    return dot(ah, bh) + (dot(ah, bl) + dot(al, bh))


def step_width(c):
    return math.gcd(WIDTHS[c], OFFSETS[c], 256)


def pack_kernel(where, g_ref, out_ref):
    out_ref[...] = g_ref[:, 0]


def pack(where, grads, c, after):
    step = step_width(c)
    n, first, half = WIDTHS[c] // step, OFFSETS[c] // step, HALF // step
    return call(
        pack_kernel,
        [grads],
        [
            pl.BlockSpec(
                (4, 1, 8, ROWS, step), lambda h, i, s: (0, 1 - s[0], 0, 0, h * half + first + i)
            )
        ],
        [pl.BlockSpec((4, 8, ROWS, step), lambda h, i, s: (0, 0, 0, h * n + i))],
        [jax.ShapeDtypeStruct((4, 8, ROWS, 2 * WIDTHS[c]), BF16)],
        "pack", after, (2, n), where, micros=2.0 * WIDTHS[c] / 256,
    )


def pair_sum_kernel(where, g_ref, r_ref, up_ref, down_ref, acc_ref, own_ref):
    y = where[1]

    def total(k, rows):
        k = lax.rem(k, 4)
        return g_ref[k, 0, rows].astype(F32) + r_ref[k, rows].astype(F32)

    for rows, up, down, acc in ((slice(0, 4), 2, 3, 1), (slice(4, 8), 1, 2, 3)):
        own_ref[rows] = total(y, rows)
        up_ref[rows] = total(y + up, rows)
        down_ref[rows] = total(y + down, rows)
        acc_ref[rows] = total(y + acc, rows)


def pair_sum(where, grads, received, c, after):
    step = step_width(c)
    n, first, half = WIDTHS[c] // step, OFFSETS[c] // step, HALF // step
    return call(
        pair_sum_kernel,
        [grads, received],
        [
            pl.BlockSpec(
                (4, 1, 8, ROWS, step), lambda h, i, s: (0, s[0], 0, 0, h * half + first + i)
            ),
            pl.BlockSpec((4, 8, ROWS, step), lambda h, i, s: (0, 0, 0, h * n + i)),
        ],
        [pl.BlockSpec((8, ROWS, step), lambda h, i, s: (0, 0, h * n + i))] * 4,
        [jax.ShapeDtypeStruct((8, ROWS, 2 * WIDTHS[c]), F32)] * 4,
        "pair_sum", after, (2, n), where, micros=4.0 * WIDTHS[c] / 256,
    )


def relay_kernel(acc_up, u1_ref, acc_down, d1_ref, up_ref, down_ref):
    up_ref[...] = acc_up[...] + u1_ref[...]
    down_ref[...] = acc_down[...] + d1_ref[...]


def relay(acc, u1, d1, w, after):
    block = (2, ROWS, 2 * w)
    low = pl.BlockSpec(block, lambda i: (i, 0, 0))
    high = pl.BlockSpec(block, lambda i: (i + 2, 0, 0))
    return call(
        relay_kernel,
        [acc, u1, acc, d1],
        [low, low, high, high],
        [low, low],
        [jax.ShapeDtypeStruct((4, ROWS, 2 * w), F32)] * 2,
        "relay", after, (2,), micros=1.0,
    )


def finish_kernel(own_ref, d1_ref, u2_ref, u1_ref, d2_ref, out_ref):
    def write(a_ref, b_ref):
        total = own_ref[...] + (a_ref[...] + b_ref[...])
        for j in range(4):
            out_ref[2 * j] = total[j]
            out_ref[2 * j + 1] = total[j]

    pl.when(pl.program_id(0) == 0)(lambda: write(d1_ref, u2_ref))
    pl.when(pl.program_id(0) == 1)(lambda: write(u1_ref, d2_ref))


def finish(own, d1, u2, u1, d2, w, after):
    block = (4, ROWS, 2 * w)
    held = pl.BlockSpec(block, lambda i: (0, 0, 0))
    return call(
        finish_kernel,
        [own, d1, u2, u1, d2],
        [
            pl.BlockSpec(block, lambda i: (i, 0, 0)),
            held,
            held,
            pl.BlockSpec(block, lambda i: (1, 0, 0)),
            held,
        ],
        [pl.BlockSpec((8, ROWS, 2 * w), lambda i: (i, 0, 0))],
        [jax.ShapeDtypeStruct((16, ROWS, 2 * w), F32)],
        "finish", after, (2,), micros=1.0,
    )


def step_of(gradient, momentum):
    renewed = decay_rate * momentum + gradient
    return renewed, gradient + decay_rate * renewed


def add_gram(total_ref, before_ref, own, other):
    high, low = split(jnp.concatenate([own, other], axis=1))
    for i in range(3):
        rows = slice(i * 256, (i + 1) * 256)
        block = dot3(high[rows], low[rows], high, low, NT)
        total_ref[rows] = block if before_ref is None else before_ref[rows] + block


def nesterov_kernel(where, g_ref, gp_ref, m_ref, mp_ref, *refs):
    new_ref, own_ref, other_ref, total_ref = refs[-4:]
    new_ref[...], own = step_of(g_ref[...], m_ref[...])
    other = step_of(gp_ref[...], mp_ref[...])[1]
    own_ref[...], other_ref[...] = own, other
    first = pl.program_id(0) == 0
    before = refs[0] if len(refs) > 4 else None
    pl.when(first)(lambda: add_gram(total_ref, before, own, other))
    pl.when(jnp.logical_not(first))(lambda: add_gram(total_ref, total_ref, own, other))


def nesterov(where, gradient, momentum, partner, state, c, after):
    step = step_width(c)
    n, first = WIDTHS[c] // step, OFFSETS[c] // step
    block = (HID, step)
    mine = pl.BlockSpec(block, lambda i, s: (0, s[2] * n + i))
    theirs = pl.BlockSpec(block, lambda i, s: (0, (1 - s[2]) * n + i))
    place = pl.BlockSpec(block, lambda i, s: (0, first + i))
    whole = pl.BlockSpec((HID, HID), lambda i, s: (0, 0))
    wide = jax.ShapeDtypeStruct((HID, HALF), F32)
    carried = [] if state is None else [state[3], state[0], state[1], state[2]]
    return call(
        nesterov_kernel,
        [gradient, gradient, momentum, partner] + carried,
        [mine, theirs, place, place]
        + ([whole] + [pl.BlockSpec(memory_space=pl.ANY)] * 3 if carried else []),
        [place, place, place, whole],
        [wide, wide, wide, jax.ShapeDtypeStruct((HID, HID), F32)],
        "nesterov", after, (n,), where,
        aliases={5: 0, 6: 1, 7: 2} if carried else {},
        micros=6.0,
    )


def solve_kernel(where, g_ref, gp_ref, m_ref, mp_ref, before_ref, *refs):
    own_refs, other_refs, refs = refs[:4], refs[4:8], refs[9:]
    new_ref, out_ref, gram_ref, last_own, last_other, *scratch = refs
    h = where[2]
    pairs = [scratch[2 * i : 2 * i + 2] for i in range(4)]

    new_ref[...], own = step_of(g_ref[...], m_ref[...])
    other = step_of(gp_ref[...], mp_ref[...])[1]
    last_own[...], last_other[...] = own, other
    add_gram(gram_ref, before_ref, own, other)

    eye = lax.broadcasted_iota(jnp.int32, (HID, HID), 0) == lax.broadcasted_iota(
        jnp.int32, (HID, HID), 1
    )
    gram_block = gram_ref[...]
    squares = jnp.sum(jnp.where(eye, gram_block, 0.0), axis=(0, 1), keepdims=True)
    inverse = 1.0 / (jnp.sqrt(squares) + norm_epsilon)
    a, p, s, q = pairs
    a[0][...], a[1][...] = split(gram_block * (inverse * inverse))

    def multiply(x, y, to, poly=None):
        for i in range(3):
            rows = slice(i * 256, (i + 1) * 256)
            for j in range(i, 3):
                cols = slice(j * 256, (j + 1) * 256)
                value = dot3(x[0][rows], x[1][rows], y[0][:, cols], y[1][:, cols], NN)
                if poly is not None:
                    base = poly[0][rows, cols].astype(F32) + poly[1][rows, cols].astype(F32)
                    value = sq_term * base + cube_term * value
                    if i == j:
                        value = value + jnp.where(eye[:256, :256], lin_term, 0.0)
                high, low = split(value)
                to[0][rows, cols], to[1][rows, cols] = high, low
                if j > i:
                    to[0][cols, rows], to[1][cols, rows] = high.T, low.T

    multiply(a, a, p, a)
    multiply(p, a, s)
    multiply(p, s, a)
    multiply(a, a, s, a)
    multiply(s, p, q)
    multiply(s, a, p)
    multiply(s, p, a)
    multiply(a, a, s, a)
    multiply(s, q, p)

    scale = inverse * (rms_match * math.sqrt(max(HID, D)))
    in_last = 256 * 3 + LANES * h >= OFFSETS[-1]
    column = pl.multiple_of(256 * 3 + LANES * h - OFFSETS[-1], LANES) if WIDTHS[-1] > LANES else 0
    for k in range(4):
        own, other = own_refs[k][...], other_refs[k][...]
        if k == 3:
            here = pl.ds(column, LANES)
            own = jnp.where(in_last, last_own[:, here], own)
            other = jnp.where(in_last, last_other[:, here], other)
        high, low = split(jnp.concatenate([own, other], axis=1))
        for i in range(3):
            rows = slice(i * 256, (i + 1) * 256)
            value = dot3(p[0][rows], p[1][rows], high, low, NN) * scale
            value = value.astype(BF16)
            out_ref[4 * h + k, rows] = value[:, :LANES]
            out_ref[4 * (1 - h) + k, rows] = value[:, LANES:]


def solve(where, gradient, momentum, partner, state):
    c = len(WIDTHS) - 1
    w = WIDTHS[c]
    block = (HID, w)
    place = pl.BlockSpec(block, lambda i, s: (0, OFFSETS[c] // w))
    whole = pl.BlockSpec((HID, HID), lambda i, s: (0, 0))
    columns = [
        pl.BlockSpec((HID, LANES), lambda i, s, k=k: (0, 2 * k + s[2])) for k in range(4)
    ]
    renewed, own, other, total = state
    return call(
        solve_kernel,
        [gradient, gradient, momentum, partner, total] + [own] * 4 + [other] * 4 + [renewed],
        [
            pl.BlockSpec(block, lambda i, s: (0, s[2])),
            pl.BlockSpec(block, lambda i, s: (0, 1 - s[2])),
            place,
            place,
            whole,
            *columns,
            *columns,
            pl.BlockSpec(memory_space=pl.ANY),
        ],
        [place, pl.BlockSpec((8, HID, LANES), lambda i, s: (0, 0, 0))],
        [
            jax.ShapeDtypeStruct((HID, HALF), F32),
            jax.ShapeDtypeStruct((8, HID, LANES), BF16),
        ],
        "solve", (), (1,), where,
        aliases={13: 0},
        scratch=[pltpu.VMEM((HID, HID), F32)]
        + [pltpu.VMEM(block, F32)] * 2
        + [pltpu.VMEM((HID, HID), BF16)] * 8,
        micros=40.0,
    )


def join_kernel(x_ref, out_ref):
    for h in range(2):
        out_ref[:, :, h * LANES : (h + 1) * LANES] = x_ref[:, h]


def join(blocks):
    out, _ = call(
        join_kernel,
        [blocks],
        [pl.BlockSpec((16, 2, ROWS, LANES), lambda i: (i, 0, 0, 0))],
        [pl.BlockSpec((16, ROWS, 2 * LANES), lambda i: (i, 0, 0))],
        [jax.ShapeDtypeStruct((64, ROWS, 2 * LANES), BF16)],
        "join", grid=(4,),
    )
    return out


def body(grad_parts, momentum):
    dp, ex = lax.axis_index("dp"), lax.axis_index("expert")
    where = jnp.stack([dp % 2, dp // 2, ex % 2]).astype(jnp.int32)
    grads = grad_parts.reshape(4, 2, 8, ROWS, D)
    momentum = momentum[0]
    core = [(i, i ^ 1) for i in range(8)]
    upward = [(i, (i + 2) % 8) for i in range(8)]
    downward = [(i, (i - 2) % 8) for i in range(8)]
    partner = [(i, i ^ 1) for i in range(16)]
    n = len(WIDTHS)
    theirs = lax.ppermute(momentum, "expert", partner)
    received, sums, first, second, moved, token = ({} for _ in range(6))

    def after(*steps):
        return [token[step] for step in steps if step in token]

    def do_pack(c, *waits):
        out, token["pack", c] = pack(where, grads, c, after(*waits))
        received[c] = lax.ppermute(out, "dp", core)

    def do_sum(c, *waits):
        *sums[c], token["sum", c] = pair_sum(where, grads, received[c], c, after(*waits))
        up, down = sums[c][:2]
        first[c] = (lax.ppermute(up, "dp", upward), lax.ppermute(down, "dp", downward))

    def do_relay(c, *waits):
        up, down, token["relay", c] = relay(sums[c][2], *first[c], WIDTHS[c], after(*waits))
        second[c] = (lax.ppermute(up, "dp", upward), lax.ppermute(down, "dp", downward))

    def do_finish(c, *waits, arrays=()):
        out, token["finish", c] = finish(
            sums[c][3], first[c][1], second[c][0], first[c][0], second[c][1], WIDTHS[c],
            after(*waits) + list(arrays),
        )
        out = lax.all_to_all(out, "expert", split_axis=0, concat_axis=0, tiled=True)
        moved[c] = out.reshape(HID, -1)

    def do_nesterov(c, *waits):
        *state[:], token["nesterov", c] = nesterov(
            where, moved[c], momentum, theirs, state or None, c, after(*waits)
        )

    state = []
    do_pack(0)
    do_pack(1)
    do_sum(0)
    do_sum(1)
    do_pack(2)
    do_relay(0, ("sum", 1), ("pack", 2))
    do_sum(2, ("relay", 0))
    for c in range(n):
        if c + 3 < n:
            do_pack(c + 3, ("sum", c + 2))
        if c + 1 < n:
            do_relay(c + 1, ("sum", c + 2), ("pack", c + 3), ("finish", c - 1))
        if c + 3 < n:
            do_sum(c + 3, ("relay", c + 1))
        last = () if c == n - 1 else (("nesterov", c - 2),)
        do_finish(c, ("sum", c + 3), ("relay", c + 1), *last, arrays=[theirs] if c == 1 else ())
        if c > 0:
            do_nesterov(c - 1, ("finish", c))
    renewed, update, _ = solve(where, moved[n - 1], momentum, theirs, state)
    update = lax.all_to_all(
        update.reshape(128, ROWS, LANES), ("dp", "expert"), split_axis=0, concat_axis=0, tiled=True
    )
    return join(update.reshape(64, 2, ROWS, LANES)), renewed[None]


def solution(mesh):
    return jax.shard_map(
        body,
        mesh=mesh,
        in_specs=(P("dp", None, "expert", None), P(("dp", "expert"), None, None)),
        out_specs=(P(None, "expert", "dp"), P(("dp", "expert"), None, None)),
        check_vma=False,
    )
```

```python
import functools
import math

import jax
import jax.numpy as jnp
from jax import lax
from jax.experimental import pallas as pl
from jax.experimental.pallas import tpu as pltpu
from jax.sharding import PartitionSpec as P

D = 2048
HID = 768
HALF = D // 2
ROWS = 48
LANES = 128

decay_rate = 0.95
norm_epsilon = 1e-07
rms_match = 0.2
lin_term = 3.4445
sq_term = -4.775
cube_term = 2.0315

WIDTHS = (384, 256, 256, 128)
OFFSETS = tuple(sum(WIDTHS[:c]) for c in range(len(WIDTHS)))

F32 = jnp.float32
BF16 = jnp.bfloat16
MIB = 1 << 20


def call(kernel, inputs, in_specs, out_specs, out_shape, name,
         after=(), grid=(), where=None, aliases=None, scratch=(), mib=50):
    n, extra, outs = len(inputs), len(after), len(out_shape)
    lead = 0 if where is None else 1

    def run(*refs):
        first = lead + n + extra
        refs[first + outs][...] = jnp.zeros((8, LANES), F32)
        kernel(*refs[: lead + n], *refs[first : first + outs], *refs[first + outs + 1 :])

    spec = pltpu.PrefetchScalarGridSpec(
        num_scalar_prefetch=lead,
        grid=grid,
        in_specs=list(in_specs) + [pl.BlockSpec(memory_space=pl.ANY)] * extra,
        out_specs=list(out_specs) + [pl.BlockSpec((8, LANES), lambda *_: (0, 0))],
        scratch_shapes=scratch,
    )
    return pl.pallas_call(
        run,
        grid_spec=spec,
        out_shape=list(out_shape) + [jax.ShapeDtypeStruct((8, LANES), F32)],
        input_output_aliases={lead + k: v for k, v in (aliases or {}).items()},
        compiler_params=pltpu.CompilerParams(vmem_limit_bytes=mib * MIB),
        name=name,
    )(*(() if where is None else (where,)), *inputs, *after)


def split(x):
    high = x.astype(BF16)
    return high, (x - high.astype(F32)).astype(BF16)


NN = (((1,), (0,)), ((), ()))
NT = (((1,), (1,)), ((), ()))


def dot3(ah, al, bh, bl, dims):
    dot = functools.partial(lax.dot_general, dimension_numbers=dims, preferred_element_type=F32)
    return dot(ah, bh) + (dot(ah, bl) + dot(al, bh))


def step_width(c):
    return math.gcd(WIDTHS[c], OFFSETS[c], 256)


def widen_kernel(g_ref, out_ref):
    out_ref[...] = g_ref[...].astype(F32)


def widen(grads, c, after):
    step = step_width(c)
    n, first, half = WIDTHS[c] // step, OFFSETS[c] // step, HALF // step
    block = (32, ROWS, step)
    return call(
        widen_kernel,
        [grads],
        [pl.BlockSpec(block, lambda m, h, i: (m, 0, h * half + first + i))],
        [pl.BlockSpec(block, lambda m, h, i: (m, 0, h * n + i))],
        [jax.ShapeDtypeStruct((64, ROWS, 2 * WIDTHS[c]), F32)],
        "widen", after, (2, 2, n),
    )


def double_kernel(g_ref, out_ref):
    for j in range(4):
        out_ref[2 * j] = g_ref[j]
        out_ref[2 * j + 1] = g_ref[j]


def double(summed, w, after):
    return call(
        double_kernel,
        [summed],
        [pl.BlockSpec((4, ROWS, 2 * w), lambda i: (i, 0, 0))],
        [pl.BlockSpec((8, ROWS, 2 * w), lambda i: (i, 0, 0))],
        [jax.ShapeDtypeStruct((16, ROWS, 2 * w), F32)],
        "double", after, (2,),
    )


def step_of(gradient, momentum):
    renewed = decay_rate * momentum + gradient
    return renewed, gradient + decay_rate * renewed


def add_gram(total_ref, before_ref, own, other):
    high, low = split(jnp.concatenate([own, other], axis=1))
    for i in range(3):
        rows = slice(i * 256, (i + 1) * 256)
        block = dot3(high[rows], low[rows], high, low, NT)
        total_ref[rows] = block if before_ref is None else before_ref[rows] + block


def nesterov_kernel(where, g_ref, gp_ref, m_ref, mp_ref, *refs):
    new_ref, own_ref, other_ref, total_ref = refs[-4:]
    new_ref[...], own = step_of(g_ref[...], m_ref[...])
    other = step_of(gp_ref[...], mp_ref[...])[1]
    own_ref[...], other_ref[...] = own, other
    first = pl.program_id(0) == 0
    before = refs[0] if len(refs) > 4 else None
    pl.when(first)(lambda: add_gram(total_ref, before, own, other))
    pl.when(jnp.logical_not(first))(lambda: add_gram(total_ref, total_ref, own, other))


def nesterov(where, gradient, momentum, partner, state, c, after):
    step = step_width(c)
    n, first = WIDTHS[c] // step, OFFSETS[c] // step
    block = (HID, step)
    mine = pl.BlockSpec(block, lambda i, s: (0, s[0] * n + i))
    theirs = pl.BlockSpec(block, lambda i, s: (0, (1 - s[0]) * n + i))
    place = pl.BlockSpec(block, lambda i, s: (0, first + i))
    whole = pl.BlockSpec((HID, HID), lambda i, s: (0, 0))
    wide = jax.ShapeDtypeStruct((HID, HALF), F32)
    carried = [] if state is None else [state[3], state[0], state[1], state[2]]
    return call(
        nesterov_kernel,
        [gradient, gradient, momentum, partner] + carried,
        [mine, theirs, place, place]
        + ([whole] + [pl.BlockSpec(memory_space=pl.ANY)] * 3 if carried else []),
        [place, place, place, whole],
        [wide, wide, wide, jax.ShapeDtypeStruct((HID, HID), F32)],
        "nesterov", after, (n,), where,
        aliases={5: 0, 6: 1, 7: 2} if carried else {},
    )


def solve_kernel(where, g_ref, gp_ref, m_ref, mp_ref, before_ref, *refs):
    own_refs, other_refs, refs = refs[:4], refs[4:8], refs[9:]
    new_ref, out_ref, gram_ref, last_own, last_other, *scratch = refs
    h = where[0]
    pairs = [scratch[2 * i : 2 * i + 2] for i in range(4)]

    new_ref[...], own = step_of(g_ref[...], m_ref[...])
    other = step_of(gp_ref[...], mp_ref[...])[1]
    last_own[...], last_other[...] = own, other
    add_gram(gram_ref, before_ref, own, other)

    eye = lax.broadcasted_iota(jnp.int32, (HID, HID), 0) == lax.broadcasted_iota(
        jnp.int32, (HID, HID), 1
    )
    gram_block = gram_ref[...]
    squares = jnp.sum(jnp.where(eye, gram_block, 0.0), axis=(0, 1), keepdims=True)
    inverse = 1.0 / (jnp.sqrt(squares) + norm_epsilon)
    a, p, s, q = pairs
    a[0][...], a[1][...] = split(gram_block * (inverse * inverse))

    def multiply(x, y, to, poly=None):
        for i in range(3):
            rows = slice(i * 256, (i + 1) * 256)
            for j in range(i, 3):
                cols = slice(j * 256, (j + 1) * 256)
                value = dot3(x[0][rows], x[1][rows], y[0][:, cols], y[1][:, cols], NN)
                if poly is not None:
                    base = poly[0][rows, cols].astype(F32) + poly[1][rows, cols].astype(F32)
                    value = sq_term * base + cube_term * value
                    if i == j:
                        value = value + jnp.where(eye[:256, :256], lin_term, 0.0)
                high, low = split(value)
                to[0][rows, cols], to[1][rows, cols] = high, low
                if j > i:
                    to[0][cols, rows], to[1][cols, rows] = high.T, low.T

    multiply(a, a, p, a)
    multiply(p, a, s)
    multiply(p, s, a)
    multiply(a, a, s, a)
    multiply(s, p, q)
    multiply(s, a, p)
    multiply(s, p, a)
    multiply(a, a, s, a)
    multiply(s, q, p)

    scale = inverse * (rms_match * math.sqrt(max(HID, D)))
    in_last = 256 * 3 + LANES * h >= OFFSETS[-1]
    column = pl.multiple_of(256 * 3 + LANES * h - OFFSETS[-1], LANES) if WIDTHS[-1] > LANES else 0
    for k in range(4):
        own, other = own_refs[k][...], other_refs[k][...]
        if k == 3:
            here = pl.ds(column, LANES)
            own = jnp.where(in_last, last_own[:, here], own)
            other = jnp.where(in_last, last_other[:, here], other)
        high, low = split(jnp.concatenate([own, other], axis=1))
        for i in range(3):
            rows = slice(i * 256, (i + 1) * 256)
            value = dot3(p[0][rows], p[1][rows], high, low, NN) * scale
            value = value.astype(BF16)
            out_ref[4 * h + k, rows] = value[:, :LANES]
            out_ref[4 * (1 - h) + k, rows] = value[:, LANES:]


def solve(where, gradient, momentum, partner, state):
    c = len(WIDTHS) - 1
    w = WIDTHS[c]
    block = (HID, w)
    place = pl.BlockSpec(block, lambda i, s: (0, OFFSETS[c] // w))
    whole = pl.BlockSpec((HID, HID), lambda i, s: (0, 0))
    columns = [
        pl.BlockSpec((HID, LANES), lambda i, s, k=k: (0, 2 * k + s[0])) for k in range(4)
    ]
    renewed, own, other, total = state
    return call(
        solve_kernel,
        [gradient, gradient, momentum, partner, total] + [own] * 4 + [other] * 4 + [renewed],
        [
            pl.BlockSpec(block, lambda i, s: (0, s[0])),
            pl.BlockSpec(block, lambda i, s: (0, 1 - s[0])),
            place,
            place,
            whole,
            *columns,
            *columns,
            pl.BlockSpec(memory_space=pl.ANY),
        ],
        [place, pl.BlockSpec((8, HID, LANES), lambda i, s: (0, 0, 0))],
        [
            jax.ShapeDtypeStruct((HID, HALF), F32),
            jax.ShapeDtypeStruct((8, HID, LANES), BF16),
        ],
        "solve", (), (1,), where,
        aliases={13: 0},
        scratch=[pltpu.VMEM((HID, HID), F32)]
        + [pltpu.VMEM(block, F32)] * 2
        + [pltpu.VMEM((HID, HID), BF16)] * 8,
    )


def join_kernel(x_ref, out_ref):
    for h in range(2):
        out_ref[:, :, h * LANES : (h + 1) * LANES] = x_ref[:, h]


def join(blocks):
    out, _ = call(
        join_kernel,
        [blocks],
        [pl.BlockSpec((16, 2, ROWS, LANES), lambda i: (i, 0, 0, 0))],
        [pl.BlockSpec((16, ROWS, 2 * LANES), lambda i: (i, 0, 0))],
        [jax.ShapeDtypeStruct((64, ROWS, 2 * LANES), BF16)],
        "join", grid=(4,),
    )
    return out


def body(grad_parts, momentum):
    where = jnp.full((1,), lax.axis_index("expert") % 2, jnp.int32)
    grads = grad_parts[0]
    momentum = momentum[0]
    n = len(WIDTHS)
    theirs = lax.ppermute(momentum, "expert", [(i, i ^ 1) for i in range(16)])
    sums, moved, token = {}, {}, {}
    state = []

    def after(*steps):
        return [token[step] for step in steps if step in token]

    def do_scatter(c, *waits):
        out, token["widen", c] = widen(grads, c, after(*waits))
        sums[c] = lax.psum_scatter(out, "dp", scatter_dimension=0, tiled=True)

    def do_move(c, *waits):
        out, token["double", c] = double(sums[c], WIDTHS[c], after(*waits))
        out = lax.all_to_all(out, "expert", split_axis=0, concat_axis=0, tiled=True)
        moved[c] = out.reshape(HID, -1)

    def do_nesterov(c, *waits):
        *state[:], token["nesterov", c] = nesterov(
            where, moved[c], momentum, theirs, state or None, c, after(*waits)
        )

    do_scatter(0)
    do_scatter(1, ("widen", 0))
    do_scatter(2, ("widen", 1))
    do_scatter(3, ("widen", 2))
    for c in range(n):
        do_move(c, ("nesterov", c - 2))
        if c > 0:
            do_nesterov(c - 1, ("double", c))
    renewed, update, _ = solve(where, moved[n - 1], momentum, theirs, state)
    update = lax.all_to_all(
        update.reshape(128, ROWS, LANES), ("dp", "expert"), split_axis=0, concat_axis=0, tiled=True
    )
    return join(update.reshape(64, 2, ROWS, LANES)), renewed[None]


def solution(mesh):
    return jax.shard_map(
        body,
        mesh=mesh,
        in_specs=(P("dp", None, "expert", None), P(("dp", "expert"), None, None)),
        out_specs=(P(None, "expert", "dp"), P(("dp", "expert"), None, None)),
        check_vma=False,
    )
```

```python
import functools
import math

import jax
import jax.numpy as jnp
from jax import lax
from jax.experimental import pallas as pl
from jax.experimental.pallas import tpu as pltpu
from jax.sharding import PartitionSpec as P

D = 2048
HID = 768
HALF = D // 2
ROWS = 48
LANES = 128

decay_rate = 0.95
norm_epsilon = 1e-07
rms_match = 0.2
lin_term = 3.4445
sq_term = -4.775
cube_term = 2.0315

WIDTHS = (256, 256, 256, 256)
OFFSETS = tuple(sum(WIDTHS[:c]) for c in range(len(WIDTHS)))

F32 = jnp.float32
BF16 = jnp.bfloat16
MIB = 1 << 20


def call(kernel, inputs, in_specs, out_specs, out_shape, name,
         after=(), grid=(), where=None, aliases=None, scratch=(), micros=2.0):
    n, extra, outs = len(inputs), len(after), len(out_shape)
    lead = 0 if where is None else 1

    def run(*refs):
        first = lead + n + extra
        refs[first + outs][...] = jnp.zeros((8, LANES), F32)
        kernel(*refs[: lead + n], *refs[first : first + outs], *refs[first + outs + 1 :])

    spec = pltpu.PrefetchScalarGridSpec(
        num_scalar_prefetch=lead,
        grid=grid,
        in_specs=list(in_specs) + [pl.BlockSpec(memory_space=pl.ANY)] * extra,
        out_specs=list(out_specs) + [pl.BlockSpec((8, LANES), lambda *_: (0, 0))],
        scratch_shapes=scratch,
    )
    return pl.pallas_call(
        run,
        grid_spec=spec,
        out_shape=list(out_shape) + [jax.ShapeDtypeStruct((8, LANES), F32)],
        input_output_aliases={lead + k: v for k, v in (aliases or {}).items()},
        compiler_params=pltpu.CompilerParams(vmem_limit_bytes=50 * MIB),
        cost_estimate=pl.CostEstimate(
            flops=0, bytes_accessed=int(micros * 10), transcendentals=0
        ),
        name=name,
    )(*(() if where is None else (where,)), *inputs, *after)


def split(x):
    high = x.astype(BF16)
    return high, (x - high.astype(F32)).astype(BF16)


NN = (((1,), (0,)), ((), ()))
NT = (((1,), (1,)), ((), ()))


def dot3(ah, al, bh, bl, dims):
    dot = functools.partial(lax.dot_general, dimension_numbers=dims, preferred_element_type=F32)
    return dot(ah, bh) + (dot(ah, bl) + dot(al, bh))


def step_width(c):
    return math.gcd(WIDTHS[c], OFFSETS[c], 256)


def pack_kernel(where, g_ref, out_ref):
    out_ref[...] = g_ref[:, 0]


def pack(where, grads, c, after):
    step = step_width(c)
    n, first, half = WIDTHS[c] // step, OFFSETS[c] // step, HALF // step
    return call(
        pack_kernel,
        [grads],
        [
            pl.BlockSpec(
                (4, 1, 8, ROWS, step), lambda h, i, s: (0, 1 - s[0], 0, 0, h * half + first + i)
            )
        ],
        [pl.BlockSpec((4, 8, ROWS, step), lambda h, i, s: (0, 0, 0, h * n + i))],
        [jax.ShapeDtypeStruct((4, 8, ROWS, 2 * WIDTHS[c]), BF16)],
        "pack", after, (2, n), where, micros=2.0 * WIDTHS[c] / 256,
    )


def pair_sum_kernel(where, g_ref, r_ref, up_ref, down_ref, acc_ref, own_ref):
    y = where[1]

    def total(k, rows):
        k = lax.rem(k, 4)
        return g_ref[k, 0, rows].astype(F32) + r_ref[k, rows].astype(F32)

    for rows, up, down, acc in ((slice(0, 4), 2, 3, 1), (slice(4, 8), 1, 2, 3)):
        own_ref[rows] = total(y, rows)
        up_ref[rows] = total(y + up, rows)
        down_ref[rows] = total(y + down, rows)
        acc_ref[rows] = total(y + acc, rows)


def pair_sum(where, grads, received, c, after):
    step = step_width(c)
    n, first, half = WIDTHS[c] // step, OFFSETS[c] // step, HALF // step
    return call(
        pair_sum_kernel,
        [grads, received],
        [
            pl.BlockSpec(
                (4, 1, 8, ROWS, step), lambda h, i, s: (0, s[0], 0, 0, h * half + first + i)
            ),
            pl.BlockSpec((4, 8, ROWS, step), lambda h, i, s: (0, 0, 0, h * n + i)),
        ],
        [pl.BlockSpec((8, ROWS, step), lambda h, i, s: (0, 0, h * n + i))] * 4,
        [jax.ShapeDtypeStruct((8, ROWS, 2 * WIDTHS[c]), F32)] * 4,
        "pair_sum", after, (2, n), where, micros=4.0 * WIDTHS[c] / 256,
    )


def relay_kernel(acc_up, u1_ref, acc_down, d1_ref, up_ref, down_ref):
    up_ref[...] = acc_up[...] + u1_ref[...]
    down_ref[...] = acc_down[...] + d1_ref[...]


def relay(acc, u1, d1, w, after):
    block = (2, ROWS, 2 * w)
    low = pl.BlockSpec(block, lambda i: (i, 0, 0))
    high = pl.BlockSpec(block, lambda i: (i + 2, 0, 0))
    return call(
        relay_kernel,
        [acc, u1, acc, d1],
        [low, low, high, high],
        [low, low],
        [jax.ShapeDtypeStruct((4, ROWS, 2 * w), F32)] * 2,
        "relay", after, (2,), micros=1.0,
    )


def finish_kernel(own_ref, d1_ref, u2_ref, u1_ref, d2_ref, out_ref):
    def write(a_ref, b_ref):
        total = own_ref[...] + (a_ref[...] + b_ref[...])
        for j in range(4):
            out_ref[2 * j] = total[j]
            out_ref[2 * j + 1] = total[j]

    pl.when(pl.program_id(0) == 0)(lambda: write(d1_ref, u2_ref))
    pl.when(pl.program_id(0) == 1)(lambda: write(u1_ref, d2_ref))


def finish(own, d1, u2, u1, d2, w, after):
    block = (4, ROWS, 2 * w)
    held = pl.BlockSpec(block, lambda i: (0, 0, 0))
    return call(
        finish_kernel,
        [own, d1, u2, u1, d2],
        [
            pl.BlockSpec(block, lambda i: (i, 0, 0)),
            held,
            held,
            pl.BlockSpec(block, lambda i: (1, 0, 0)),
            held,
        ],
        [pl.BlockSpec((8, ROWS, 2 * w), lambda i: (i, 0, 0))],
        [jax.ShapeDtypeStruct((16, ROWS, 2 * w), F32)],
        "finish", after, (2,), micros=1.0,
    )


def step_of(gradient, momentum):
    renewed = decay_rate * momentum + gradient
    return renewed, gradient + decay_rate * renewed


def add_gram(total_ref, before_ref, own, other):
    high, low = split(jnp.concatenate([own, other], axis=1))
    for i in range(3):
        rows = slice(i * 256, (i + 1) * 256)
        block = dot3(high[rows], low[rows], high, low, NT)
        total_ref[rows] = block if before_ref is None else before_ref[rows] + block


def nesterov_kernel(where, g_ref, gp_ref, m_ref, mp_ref, *refs):
    new_ref, own_ref, other_ref, total_ref = refs[-4:]
    new_ref[...], own = step_of(g_ref[...], m_ref[...])
    other = step_of(gp_ref[...], mp_ref[...])[1]
    own_ref[...], other_ref[...] = own, other
    first = pl.program_id(0) == 0
    before = refs[0] if len(refs) > 4 else None
    pl.when(first)(lambda: add_gram(total_ref, before, own, other))
    pl.when(jnp.logical_not(first))(lambda: add_gram(total_ref, total_ref, own, other))


def nesterov(where, gradient, momentum, partner, state, c, after):
    step = step_width(c)
    n, first = WIDTHS[c] // step, OFFSETS[c] // step
    block = (HID, step)
    mine = pl.BlockSpec(block, lambda i, s: (0, s[2] * n + i))
    theirs = pl.BlockSpec(block, lambda i, s: (0, (1 - s[2]) * n + i))
    place = pl.BlockSpec(block, lambda i, s: (0, first + i))
    whole = pl.BlockSpec((HID, HID), lambda i, s: (0, 0))
    wide = jax.ShapeDtypeStruct((HID, HALF), F32)
    carried = [] if state is None else [state[3], state[0], state[1], state[2]]
    return call(
        nesterov_kernel,
        [gradient, gradient, momentum, partner] + carried,
        [mine, theirs, place, place]
        + ([whole] + [pl.BlockSpec(memory_space=pl.ANY)] * 3 if carried else []),
        [place, place, place, whole],
        [wide, wide, wide, jax.ShapeDtypeStruct((HID, HID), F32)],
        "nesterov", after, (n,), where,
        aliases={5: 0, 6: 1, 7: 2} if carried else {},
        micros=6.0,
    )


def solve_kernel(where, g_ref, gp_ref, m_ref, mp_ref, before_ref, *refs):
    own_refs, other_refs, refs = refs[:4], refs[4:8], refs[9:]
    new_ref, out_ref, gram_ref, last_own, last_other, *scratch = refs
    h = where[2]
    pairs = [scratch[2 * i : 2 * i + 2] for i in range(4)]

    new_ref[...], own = step_of(g_ref[...], m_ref[...])
    other = step_of(gp_ref[...], mp_ref[...])[1]
    last_own[...], last_other[...] = own, other
    add_gram(gram_ref, before_ref, own, other)

    eye = lax.broadcasted_iota(jnp.int32, (HID, HID), 0) == lax.broadcasted_iota(
        jnp.int32, (HID, HID), 1
    )
    gram_block = gram_ref[...]
    squares = jnp.sum(jnp.where(eye, gram_block, 0.0), axis=(0, 1), keepdims=True)
    inverse = 1.0 / (jnp.sqrt(squares) + norm_epsilon)
    a, p, s, q = pairs
    a[0][...], a[1][...] = split(gram_block * (inverse * inverse))

    def multiply(x, y, to, poly=None):
        for i in range(3):
            rows = slice(i * 256, (i + 1) * 256)
            for j in range(i, 3):
                cols = slice(j * 256, (j + 1) * 256)
                value = dot3(x[0][rows], x[1][rows], y[0][:, cols], y[1][:, cols], NN)
                if poly is not None:
                    base = poly[0][rows, cols].astype(F32) + poly[1][rows, cols].astype(F32)
                    value = sq_term * base + cube_term * value
                    if i == j:
                        value = value + jnp.where(eye[:256, :256], lin_term, 0.0)
                high, low = split(value)
                to[0][rows, cols], to[1][rows, cols] = high, low
                if j > i:
                    to[0][cols, rows], to[1][cols, rows] = high.T, low.T

    multiply(a, a, p, a)
    multiply(p, a, s)
    multiply(p, s, a)
    multiply(a, a, s, a)
    multiply(s, p, q)
    multiply(s, a, p)
    multiply(s, p, a)
    multiply(a, a, s, a)
    multiply(s, q, p)

    scale = inverse * (rms_match * math.sqrt(max(HID, D)))
    in_last = 256 * 3 + LANES * h >= OFFSETS[-1]
    column = pl.multiple_of(256 * 3 + LANES * h - OFFSETS[-1], LANES) if WIDTHS[-1] > LANES else 0
    for k in range(4):
        own, other = own_refs[k][...], other_refs[k][...]
        if k == 3:
            here = pl.ds(column, LANES)
            own = jnp.where(in_last, last_own[:, here], own)
            other = jnp.where(in_last, last_other[:, here], other)
        high, low = split(jnp.concatenate([own, other], axis=1))
        for i in range(3):
            rows = slice(i * 256, (i + 1) * 256)
            value = dot3(p[0][rows], p[1][rows], high, low, NN) * scale
            value = value.astype(BF16)
            out_ref[4 * h + k, rows] = value[:, :LANES]
            out_ref[4 * (1 - h) + k, rows] = value[:, LANES:]


def solve(where, gradient, momentum, partner, state):
    c = len(WIDTHS) - 1
    w = WIDTHS[c]
    block = (HID, w)
    place = pl.BlockSpec(block, lambda i, s: (0, OFFSETS[c] // w))
    whole = pl.BlockSpec((HID, HID), lambda i, s: (0, 0))
    columns = [
        pl.BlockSpec((HID, LANES), lambda i, s, k=k: (0, 2 * k + s[2])) for k in range(4)
    ]
    renewed, own, other, total = state
    return call(
        solve_kernel,
        [gradient, gradient, momentum, partner, total] + [own] * 4 + [other] * 4 + [renewed],
        [
            pl.BlockSpec(block, lambda i, s: (0, s[2])),
            pl.BlockSpec(block, lambda i, s: (0, 1 - s[2])),
            place,
            place,
            whole,
            *columns,
            *columns,
            pl.BlockSpec(memory_space=pl.ANY),
        ],
        [place, pl.BlockSpec((8, HID, LANES), lambda i, s: (0, 0, 0))],
        [
            jax.ShapeDtypeStruct((HID, HALF), F32),
            jax.ShapeDtypeStruct((8, HID, LANES), BF16),
        ],
        "solve", (), (1,), where,
        aliases={13: 0},
        scratch=[pltpu.VMEM((HID, HID), F32)]
        + [pltpu.VMEM(block, F32)] * 2
        + [pltpu.VMEM((HID, HID), BF16)] * 8,
        micros=40.0,
    )


def join_kernel(x_ref, out_ref):
    for h in range(2):
        out_ref[:, :, h * LANES : (h + 1) * LANES] = x_ref[:, h]


def join(blocks):
    out, _ = call(
        join_kernel,
        [blocks],
        [pl.BlockSpec((16, 2, ROWS, LANES), lambda i: (i, 0, 0, 0))],
        [pl.BlockSpec((16, ROWS, 2 * LANES), lambda i: (i, 0, 0))],
        [jax.ShapeDtypeStruct((64, ROWS, 2 * LANES), BF16)],
        "join", grid=(4,),
    )
    return out


def body(grad_parts, momentum):
    dp, ex = lax.axis_index("dp"), lax.axis_index("expert")
    where = jnp.stack([dp % 2, dp // 2, ex % 2]).astype(jnp.int32)
    grads = grad_parts.reshape(4, 2, 8, ROWS, D)
    momentum = momentum[0]
    core = [(i, i ^ 1) for i in range(8)]
    upward = [(i, (i + 2) % 8) for i in range(8)]
    downward = [(i, (i - 2) % 8) for i in range(8)]
    partner = [(i, i ^ 1) for i in range(16)]
    n = len(WIDTHS)
    theirs = lax.ppermute(momentum, "expert", partner)
    received, sums, first, second, moved, token = ({} for _ in range(6))

    def after(*steps):
        return [token[step] for step in steps if step in token]

    def do_pack(c, *waits):
        out, token["pack", c] = pack(where, grads, c, after(*waits))
        received[c] = lax.ppermute(out, "dp", core)

    def do_sum(c, *waits):
        *sums[c], token["sum", c] = pair_sum(where, grads, received[c], c, after(*waits))
        up, down = sums[c][:2]
        first[c] = (lax.ppermute(up, "dp", upward), lax.ppermute(down, "dp", downward))

    def do_relay(c, *waits):
        up, down, token["relay", c] = relay(sums[c][2], *first[c], WIDTHS[c], after(*waits))
        second[c] = (lax.ppermute(up, "dp", upward), lax.ppermute(down, "dp", downward))

    def do_finish(c, *waits, arrays=()):
        out, token["finish", c] = finish(
            sums[c][3], first[c][1], second[c][0], first[c][0], second[c][1], WIDTHS[c],
            after(*waits) + list(arrays),
        )
        out = lax.all_to_all(out, "expert", split_axis=0, concat_axis=0, tiled=True)
        moved[c] = out.reshape(HID, -1)

    def do_nesterov(c, *waits):
        *state[:], token["nesterov", c] = nesterov(
            where, moved[c], momentum, theirs, state or None, c, after(*waits)
        )

    state = []
    do_pack(0)
    do_pack(1)
    do_sum(0)
    do_sum(1)
    do_pack(2)
    do_relay(0, ("sum", 1), ("pack", 2))
    do_sum(2, ("relay", 0))
    for c in range(n):
        if c + 3 < n:
            do_pack(c + 3, ("sum", c + 2))
        if c + 1 < n:
            do_relay(c + 1, ("sum", c + 2), ("pack", c + 3), ("finish", c - 1))
        if c + 3 < n:
            do_sum(c + 3, ("relay", c + 1))
        last = () if c == n - 1 else (("nesterov", c - 2),)
        do_finish(c, ("sum", c + 3), ("relay", c + 1), *last, arrays=([theirs] if c == 1 else []) + list(first.get(c + 2, ())))
        if c > 0:
            do_nesterov(c - 1, ("finish", c))
    renewed, update, _ = solve(where, moved[n - 1], momentum, theirs, state)
    update = lax.all_to_all(
        update.reshape(128, ROWS, LANES), ("dp", "expert"), split_axis=0, concat_axis=0, tiled=True
    )
    return join(update.reshape(64, 2, ROWS, LANES)), renewed[None]


def solution(mesh):
    return jax.shard_map(
        body,
        mesh=mesh,
        in_specs=(P("dp", None, "expert", None), P(("dp", "expert"), None, None)),
        out_specs=(P(None, "expert", "dp"), P(("dp", "expert"), None, None)),
        check_vma=False,
    )
```
